32 devices in a mesh: groups: 2 (over y), query: 4 (over x, core), ref: 4 (over z).
Axes of the slice: x: 2, y: 2, z: 4, core: 2. Of those that a mesh axis runs over, the one named last changes fastest.
Arguments:
- query_features: bfloat16 [64, 4096], P(None, ('groups', 'query', 'ref')), parts along dimension 1, may hold values from -6 to 6
- ref_features: bfloat16 [64, 65536], P(None, ('groups', 'ref', 'query')), parts along dimension 1, may hold values from -6 to 6
- query_blocks: int32 [64], P(('groups', 'query')), parts along dimension 0, may hold values from 0 to 7, as said below
- ref_blocks: int32 [1024], P(('groups', 'ref')), parts along dimension 0, may hold values from 0 to 7, as said below
- ref_labels: int32 [65536], P(('groups', 'ref')), parts along dimension 0, may hold values from 0 to 255
- cluster_pairs: int32 [48, 2], P('groups'), parts along dimension 0, may hold values from 0 to 7, as said below
Outputs:
- label_probs: float32 [4096, 256], P(('groups', 'query', 'ref')), parts along dimension 0
- query_potential: float32 [4096], P(('groups', 'query')), parts along dimension 0
- ref_potential: float32 [65536], P(('groups', 'ref')), parts along dimension 0
The draws below stay inside these ranges and needn't reach their ends.
There are 2 independent parts, one for each index of `groups`. The reference program is written for one: setup_inputs(seed, part) draws one part's arguments, and reference() takes and returns one part's arrays. A program takes and returns all parts, laid end to end along the dimension named above; each array names one. Nothing has to cross between parts.
Inputs may be any that keep to these rules, and one draw needn't show every extreme that they name: `cluster_pairs`: every cluster is named as a query cluster by some pair and as a reference cluster by some pair. `query_blocks`: every cluster holds at least one block. `ref_blocks`: every cluster holds at least one block.
All inputs are finite; a program needn't handle non-finite values.
Results may differ from the reference program's by a relative error of at most 0.0013.
Values may be sent and summed in bfloat16 or wider, within the bound.
A program may use at most 128 MiB of HBM per device.

```python
import math
import jax
import jax.numpy as jnp
from jax import lax

PCA = 64
LABELS = 256
CB = 64
CLUSTERS = 8
ITERS = 3
NQ = 2048
NR = 32768


def cover_draw(key, count):
    perm_key, rest_key = jax.random.split(key)
    perm = jax.random.permutation(perm_key, CLUSTERS).astype(jnp.int32)
    rest = jax.random.randint(rest_key, (count,), 0, CLUSTERS).astype(jnp.int32)
    index = jnp.arange(count, dtype=jnp.int32)
    return jnp.where(index < CLUSTERS, perm[jnp.minimum(index, CLUSTERS - 1)], rest)


def draw_query_blocks(key, part):
    key = jax.random.fold_in(key, 11)
    return cover_draw(key, NQ // CB)


def draw_ref_blocks(key, part):
    key = jax.random.fold_in(key, 12)
    return cover_draw(key, NR // CB)


def draw_cluster_pairs(key, part):
    key = jax.random.fold_in(key, 13)
    first_key, second_key, third_key, fourth_key = jax.random.split(key, 4)
    ids = jnp.arange(CLUSTERS, dtype=jnp.int32)
    left = jnp.stack([ids, jax.random.randint(first_key, (CLUSTERS,), 0, CLUSTERS).astype(jnp.int32)], axis=1)
    right = jnp.stack([jax.random.randint(second_key, (CLUSTERS,), 0, CLUSTERS).astype(jnp.int32), ids], axis=1)
    extra = jnp.stack([jax.random.randint(third_key, (CLUSTERS,), 0, CLUSTERS).astype(jnp.int32), jax.random.randint(fourth_key, (CLUSTERS,), 0, CLUSTERS).astype(jnp.int32)], axis=1)
    return jnp.concatenate([left, right, extra], axis=0)


def set_ends(drawn, key, least, high):
    shape = drawn.shape
    index_at = [jax.random.randint(jax.random.fold_in(key, axis), (), 0, shape[axis]) for axis in range(len(shape))]
    drawn = drawn.at[tuple(index_at)].set(least)
    longest = shape.index(max(shape))
    index_at[longest] = (index_at[longest] + 1) % shape[longest]
    return drawn.at[tuple(index_at)].set(high)


def steps_of(own_key, extent, shards, least, high):
    loudness = 1.0
    for position, shards_of in shards:
        draws = jax.random.uniform(jax.random.fold_in(jax.random.fold_in(own_key, 6), position), (shards_of,), jnp.float32, least / len(shards), high / len(shards))
        loudness = loudness * jnp.repeat(jnp.exp(draws), extent[position] // shards_of).reshape((-1,) + (1,) * (len(extent) - 1 - position))
    return loudness


def noise(key, shape, width, bound, cuts=(), kind=jnp.bfloat16):
    entries = jax.random.normal(key, shape, jnp.float32) * width
    if len(cuts) > 0:
        entries = steps_of(key, shape, cuts, -0.22, 0.18) * entries
    return jnp.clip(entries, min=-bound, max=bound).astype(kind)


def setup_inputs(seed: int = 0, part: int = 0) -> dict:
    seeds = jax.random.split(jax.random.key(seed), 7)
    own_keys = jax.random.split(jax.random.fold_in(seeds[6], part), 7)
    return {
        "query_features": noise(own_keys[0], (PCA, NQ), 1.0, 6.0, ((1, 16),)),
        "ref_features": noise(own_keys[1], (PCA, NR), 1.0, 6.0, ((1, 16),)),
        "query_blocks": draw_query_blocks(jax.random.fold_in(jax.random.fold_in(seeds[6], part), 71), part),
        "ref_blocks": draw_ref_blocks(jax.random.fold_in(jax.random.fold_in(seeds[6], part), 71), part),
        "ref_labels": set_ends(jax.random.randint(own_keys[4], (NR,), 0, LABELS), jax.random.fold_in(own_keys[4], 1), 0, LABELS - 1).astype(jnp.int32),
        "cluster_pairs": draw_cluster_pairs(jax.random.fold_in(jax.random.fold_in(seeds[6], part), 71), part),
    }


EPS = 0.002
NEG = -1.0e30


def pair_table(cluster_pairs):
    ids = jnp.arange(CLUSTERS, dtype=jnp.int32)
    first = (cluster_pairs[:, 0:1] == ids[None, :]).astype(jnp.float32)
    second = (cluster_pairs[:, 1:2] == ids[None, :]).astype(jnp.float32)
    return (jnp.dot(first.T, second, preferred_element_type=jnp.float32) > 0.5).astype(jnp.int32)


def reference(query_features, ref_features, query_blocks, ref_blocks, ref_labels, cluster_pairs):
    table = pair_table(cluster_pairs)
    query_clus = jnp.repeat(query_blocks, CB)
    ref_clus = jnp.repeat(ref_blocks, CB)
    ref_norm = jnp.sum(jnp.square(ref_features.astype(jnp.float32)), axis=0)
    row_block = math.gcd(NQ, 256)
    count = NQ // row_block
    log_query = -math.log(NQ)
    log_ref = -math.log(NR)

    def block_data(index):
        start = (index * row_block).astype(jnp.int32)
        rows = lax.dynamic_slice_in_dim(query_features, start, row_block, 1)
        cross = lax.dot_general(rows, ref_features, (((0,), (0,)), ((), ())), preferred_element_type=jnp.float32)
        rows_norm = jnp.sum(jnp.square(rows.astype(jnp.float32)), axis=0)
        cost = (rows_norm[:, None] + ref_norm[None, :] - 2.0 * cross) / PCA
        clus = lax.dynamic_slice_in_dim(query_clus, start, row_block, 0)
        allowed = table[clus[:, None], ref_clus[None, :]]
        return cost, allowed > 0, start

    blocks = jnp.arange(count, dtype=jnp.int32)
    query_pot = jnp.zeros((NQ,), jnp.float32)
    ref_pot = jnp.zeros((NR,), jnp.float32)
    for step in range(ITERS):
        def row_pass(index):
            cost, allowed, start = block_data(index)
            scores = (ref_pot[None, :] - cost) / EPS
            peak = jnp.max(jnp.where(allowed, scores, NEG), axis=1)
            mass = jnp.sum(jnp.where(allowed, jnp.exp(scores - peak[:, None]), 0.0), axis=1)
            return EPS * log_query - EPS * (peak + jnp.log(mass))

        query_pot = lax.map(row_pass, blocks).reshape(NQ)

        def column_pass(carry, index):
            cost, allowed, start = block_data(index)
            pot = lax.dynamic_slice_in_dim(query_pot, start, row_block, 0)
            scores = (pot[:, None] - cost) / EPS
            peak = jnp.max(jnp.where(allowed, scores, NEG), axis=0)
            mass = jnp.sum(jnp.where(allowed, jnp.exp(scores - peak[None, :]), 0.0), axis=0)
            top = jnp.maximum(carry[0], peak)
            total = carry[1] * jnp.exp(carry[0] - top) + mass * jnp.exp(peak - top)
            return (top, total), None

        start_carry = (jnp.full((NR,), NEG, jnp.float32), jnp.zeros((NR,), jnp.float32))
        (peak, mass), unused = lax.scan(column_pass, start_carry, blocks)
        ref_pot = EPS * log_ref - EPS * (peak + jnp.log(mass))

    onehot = (ref_labels[:, None] == jnp.arange(LABELS, dtype=jnp.int32)[None, :]).astype(jnp.bfloat16)

    def label_pass(index):
        cost, allowed, start = block_data(index)
        pot = lax.dynamic_slice_in_dim(query_pot, start, row_block, 0)
        plan = jnp.where(allowed, jnp.exp((pot[:, None] + ref_pot[None, :] - cost) / EPS), 0.0)
        totals = jnp.sum(plan, axis=1)
        label_mass = jnp.dot(plan.astype(jnp.bfloat16), onehot, preferred_element_type=jnp.float32)
        return label_mass / totals[:, None]

    label_probs = lax.map(label_pass, blocks).reshape(NQ, LABELS)
    return label_probs, query_pot, ref_pot
```

```python
import functools
import math

import jax
import jax.numpy as jnp
from jax import lax
from jax.experimental import pallas as pl
from jax.experimental.pallas import tpu as pltpu
from jax.sharding import PartitionSpec as P

PCA = 64
LABELS = 256
CB = 64
ITERS = 3
EPS = 0.002

SCALE = math.log2(math.e) / EPS
DOT_SCALE = 2.0 * SCALE / PCA
BLOCKED = -(2.0**100)
FLOOR = -1e20
TINY = 1e-37
DEPTH = 128
MESH = pl.DeviceIdType.MESH
F32 = jnp.float32
BF16 = jnp.bfloat16


def to_row(lanes, reduce):
    return reduce(lanes.T, axis=0, keepdims=True)


def from_row(row):
    return jnp.broadcast_to(row, (128, row.shape[1])).T


def kernel(
    nq, nr, q_ref, r_ref, labels_ref, qb_ref, rb_ref, pairs_ref,
    probs_ref, qpot_ref, rpot_ref,
    qg, aug_r, aug_q, scores, onehot, lanes, spread, peak, share, scale_row,
    rbuf, cbuf, lbuf, lsend,
    q_send, q_recv, r_send, r_recv, f_send, f_recv, row_send, row_recv, col_send, col_recv,
    l_send, l_recv,
):
    own_q = lax.axis_index("query")
    own_r = lax.axis_index("ref")
    qw = q_ref.shape[1]
    rw = r_ref.shape[1]
    rows_n = qw * nr
    cols_n = rw * nq
    chips = nq // 2
    core = lax.rem(own_q, 2)
    chip = own_q // 2
    sibling = chip * 2 + (1 - core)
    log_query = math.log2(rows_n * nq)
    log_ref = math.log2(cols_n * nr)

    barrier = pltpu.get_barrier_semaphore()
    for d in range(1, nq):
        pl.semaphore_signal(
            barrier, inc=1, device_id={"query": lax.rem(own_q + d, nq)}, device_id_type=MESH
        )
    for d in range(1, nr):
        pl.semaphore_signal(
            barrier, inc=1, device_id={"ref": lax.rem(own_r + d, nr)}, device_id_type=MESH
        )
    pl.semaphore_wait(barrier, nq + nr - 2)

    def block_cols(owner, width):
        return pl.ds(pl.multiple_of(owner * width, 128) if width % 128 == 0 else owner * width, width)

    own_cols = block_cols(own_r, qw)
    q_copies = []
    r_copies = []
    for d in range(1, chips):
        r_copies.append(
            pltpu.make_async_remote_copy(
                src_ref=r_ref,
                dst_ref=aug_r.at[pl.ds(0, PCA), block_cols(own_q, rw)],
                send_sem=r_send.at[d],
                recv_sem=r_recv.at[d],
                device_id={"query": lax.rem(chip + d, chips) * 2 + core},
                device_id_type=MESH,
            )
        )
        r_copies[-1].start()
    sibling_copy = pltpu.make_async_remote_copy(
        src_ref=r_ref,
        dst_ref=aug_r.at[pl.ds(0, PCA), block_cols(own_q, rw)],
        send_sem=r_send.at[0],
        recv_sem=r_recv.at[0],
        device_id={"query": sibling},
        device_id_type=MESH,
    )
    sibling_copy.start()
    for d in range(1, nr):
        q_copies.append(
            pltpu.make_async_remote_copy(
                src_ref=q_ref,
                dst_ref=qg.at[own_r],
                send_sem=q_send.at[d],
                recv_sem=q_recv.at[d],
                device_id={"ref": lax.rem(own_r + d, nr)},
                device_id_type=MESH,
            )
        )
        q_copies[-1].start()

    qg[own_r] = q_ref[...]
    aug_r[pl.ds(0, PCA), block_cols(own_q, rw)] = r_ref[...]
    aug_r[pl.ds(80, DEPTH - 80), :] = jnp.zeros((DEPTH - 80, cols_n), BF16)

    sub = lax.broadcasted_iota(jnp.int32, (8, 128), 0)
    lane = lax.broadcasted_iota(jnp.int32, (8, 128), 1)

    parts = []
    for k in range(rows_n // 128):
        cluster = jnp.where(lane < CB, qb_ref[0, 2 * k], qb_ref[0, 2 * k + 1])
        hit = jnp.zeros((8, 128), F32)
        for p in range(pairs_ref.shape[0]):
            both = jnp.logical_and(sub == pairs_ref[p, 1], cluster == pairs_ref[p, 0])
            hit = jnp.where(both, 1.0, hit)
        parts.append(jnp.where(hit > 0.5, 0.0, BLOCKED))
    blocked = jnp.concatenate(parts, axis=1)

    label_id = lax.broadcasted_iota(jnp.int32, (LABELS, 128), 0)

    def label_step(k, carry):
        cols = pl.ds(pl.multiple_of(k * 128, 128), 128)
        onehot[:, cols] = jnp.where(label_id == labels_ref[:, cols], 1.0, 0.0).astype(BF16)
        return carry

    lax.fori_loop(0, cols_n // 128, label_step, 0, unroll=2)

    for copy in q_copies:
        copy.wait()
    if qw % 128 == 0:
        q_cols = jnp.concatenate([qg[k].astype(F32) for k in range(nr)], axis=1)
    else:
        q_cols = jnp.concatenate([qg[k].astype(F32) for k in range(nr)], axis=1)
    q_norm = jnp.sum(q_cols * q_cols, axis=0, keepdims=True)
    filler = jnp.concatenate(
        [jnp.full((3, rows_n), -1.0, F32), jnp.zeros((DEPTH - PCA - 11, rows_n), F32)], axis=0
    )
    aug_q[...] = jnp.concatenate([q_cols, blocked, filler], axis=0).T.astype(BF16)

    lanes[...] = jnp.full((rows_n, 128), -3e38, F32)
    step_w = 256
    row_t = 128

    def score_block(owner):
        base = owner * rw

        def score_step(j, carry):
            cols = pl.ds(pl.multiple_of(base + j * step_w, 128), step_w)
            piece = aug_r[pl.ds(0, PCA), cols].astype(F32)
            half = 0.5 * jnp.sum(piece * piece, axis=0, keepdims=True)
            high = half.astype(BF16).astype(F32)
            middle = (half - high).astype(BF16).astype(F32)
            low = half - high - middle
            ids = []
            for t in range(step_w // 128):
                at = (base + j * step_w) // CB + 2 * t
                cluster = jnp.where(lane < CB, rb_ref[0, at], rb_ref[0, at + 1])
                ids.append(jnp.where(sub == cluster, 1.0, 0.0))
            extra = jnp.concatenate(
                [jnp.concatenate(ids, axis=1), high, middle, low, jnp.zeros((5, step_w), F32)],
                axis=0,
            )
            aug_r[pl.ds(PCA, 16), cols] = extra.astype(BF16)
            right = aug_r[:, cols]
            for i in range(rows_n // row_t):
                rows = pl.ds(i * row_t, row_t)
                value = DOT_SCALE * jnp.dot(aug_q[rows, :], right, preferred_element_type=F32)
                scores[rows, cols] = value
                top = lanes[rows, :]
                for t in range(step_w // 128):
                    top = jnp.maximum(top, value[:, t * 128 : (t + 1) * 128])
                lanes[rows, :] = top
            return carry

        lax.fori_loop(0, rw // step_w, score_step, 0)

    score_block(own_q)
    sibling_copy.wait()
    score_block(sibling)
    handed = []
    for d in range(1, chips):
        r_copies[d - 1].wait()
        owner = lax.rem(chip + chips - d, chips) * 2 + core
        block = aug_r.at[pl.ds(0, PCA), block_cols(owner, rw)]
        copy = pltpu.make_async_remote_copy(
            src_ref=block,
            dst_ref=block,
            send_sem=f_send.at[d],
            recv_sem=f_recv.at[d],
            device_id={"query": sibling},
            device_id_type=MESH,
        )
        copy.start()
        handed.append(copy)
    for d in range(1, chips):
        score_block(lax.rem(chip + chips - d, chips) * 2 + core)
    for d in range(1, chips):
        handed[d - 1].wait()
        score_block(lax.rem(chip + chips - d, chips) * 2 + 1 - core)

    def swap(buf, stage, send, recv, axis, own, count):
        copies = []
        for d in range(1, count):
            copies.append(
                pltpu.make_async_remote_copy(
                    src_ref=buf.at[stage, own],
                    dst_ref=buf.at[stage, own],
                    send_sem=send.at[stage, d],
                    recv_sem=recv.at[stage, d],
                    device_id={axis: lax.rem(own + d, count)},
                    device_id_type=MESH,
                )
            )
            copies[-1].start()
        return copies

    def swap_rows(stage, row):
        rbuf[stage, own_r] = row
        return swap(rbuf, stage, row_send, row_recv, "ref", own_r, nr)

    def swap_cols(stage, row):
        cbuf[stage, own_q] = row
        return swap(cbuf, stage, col_send, col_recv, "query", own_q, nq)

    def total_of(buf, stage, count):
        total = buf[stage, 0]
        for k in range(1, count):
            total = total + buf[stage, k]
        return total

    def joined(buf, stage, count):
        top = buf[stage, 0]
        for k in range(1, count):
            top = jnp.maximum(top, buf[stage, k])
        mass = jnp.exp2(buf[stage, 0] - top)
        for k in range(1, count):
            mass = mass + jnp.exp2(buf[stage, k] - top)
        return top, mass

    row_b = 64
    lane_steps = 8

    def row_sweep(term, bound):
        def over_rows(i, carry):
            rows = pl.ds(pl.multiple_of(i * row_b, row_b), row_b)
            held = bound[rows, :] if bound is not None else None

            def over_cols(j, acc):
                for t in range(lane_steps):
                    at = pl.multiple_of((j * lane_steps + t) * 128, 128)
                    acc = acc + term(rows, pl.ds(at, 128), held)
                return acc

            lanes[rows, :] = lax.fori_loop(
                0, cols_n // (128 * lane_steps), over_cols, jnp.zeros((row_b, 128), F32)
            )
            return carry

        lax.fori_loop(0, rows_n // row_b, over_rows, 0)
        return to_row(lanes[...], jnp.sum)

    top = jnp.maximum(to_row(lanes[...], jnp.max), FLOOR)
    spread[...] = from_row(top)
    mass = row_sweep(lambda rows, cols, held: jnp.exp2(scores[rows, cols] - held), spread)
    for copy in swap_rows(0, top + jnp.log2(jnp.maximum(mass, TINY))):
        copy.wait()
    top, mass = joined(rbuf, 0, nr)
    query_base = -log_query - (top + jnp.log2(mass))
    spread[...] = from_row(query_base)

    col_w = 256

    def column_first(j, carry):
        starts = [pl.multiple_of(j * col_w + t * 128, 128) for t in range(col_w // 128)]
        tops = [jnp.full((8, 128), FLOOR, F32) for _ in starts]
        for i in range(rows_n // row_b):
            rows = pl.ds(i * row_b, row_b)
            base = spread[rows, :]
            for t, at in enumerate(starts):
                value = scores[rows, pl.ds(at, 128)] + base
                tops[t] = jnp.maximum(
                    tops[t], jnp.max(value.reshape(row_b // 8, 8, 128), axis=0)
                )
        tops = [jnp.max(top, axis=0, keepdims=True) for top in tops]
        sums = [jnp.zeros((8, 128), F32) for _ in starts]
        for i in range(rows_n // row_b):
            rows = pl.ds(i * row_b, row_b)
            base = spread[rows, :]
            for t, at in enumerate(starts):
                value = jnp.exp2(scores[rows, pl.ds(at, 128)] + base - tops[t])
                scores[rows, pl.ds(at, 128)] = value
                sums[t] = sums[t] + jnp.sum(value.reshape(row_b // 8, 8, 128), axis=0)
        for t, at in enumerate(starts):
            peak[:, pl.ds(at, 128)] = tops[t]
            share[:, pl.ds(at, 128)] = jnp.sum(sums[t], axis=0, keepdims=True)
        return carry

    lax.fori_loop(0, cols_n // col_w, column_first, 0)
    for copy in swap_cols(0, peak[...] + jnp.log2(jnp.maximum(share[...], TINY))):
        copy.wait()
    top, mass = joined(cbuf, 0, nq)
    share[...] = jnp.exp2(peak[...] - top)
    peak[...] = top
    scale_row[...] = share[...] * (2.0**-log_ref) / mass

    for step in range(1, ITERS):
        part = row_sweep(lambda rows, cols, held: scores[rows, cols] * scale_row[:, cols], None)
        for copy in swap_rows(step, part):
            copy.wait()
        row_scale = 2.0**-log_query / total_of(rbuf, step, nr)
        spread[...] = from_row(row_scale)

        def column_later(j, carry):
            starts = [pl.multiple_of(j * col_w + t * 128, 128) for t in range(col_w // 128)]
            sums = [jnp.zeros((8, 128), F32) for _ in starts]
            for i in range(rows_n // row_b):
                rows = pl.ds(i * row_b, row_b)
                factor = spread[rows, :]
                for t, at in enumerate(starts):
                    value = scores[rows, pl.ds(at, 128)] * factor
                    sums[t] = sums[t] + jnp.sum(value.reshape(row_b // 8, 8, 128), axis=0)
            for t, at in enumerate(starts):
                scale_row[:, pl.ds(at, 128)] = jnp.sum(sums[t], axis=0, keepdims=True)
            return carry

        lax.fori_loop(0, cols_n // col_w, column_later, 0)
        for copy in swap_cols(step, share[...] * scale_row[...]):
            copy.wait()
        col_scale = 2.0**-log_ref / total_of(cbuf, step, nq)
        scale_row[...] = share[...] * col_scale

    plan_w = 512

    def label_mass(owner):
        rows = pl.ds(pl.multiple_of(owner * qw, qw), qw)
        factor = spread[rows, :]

        def over_cols(j, carry):
            acc, total = carry
            pieces = []
            for t in range(plan_w // 128):
                cols = pl.ds(pl.multiple_of(j * plan_w + t * 128, 128), 128)
                value = scores[rows, cols] * (factor * scale_row[:, cols])
                total = total + value
                pieces.append(value.astype(BF16))
            marks = onehot[:, pl.ds(pl.multiple_of(j * plan_w, 128), plan_w)]
            acc = acc + lax.dot_general(
                jnp.concatenate(pieces, axis=1),
                marks,
                (((1,), (1,)), ((), ())),
                preferred_element_type=F32,
            )
            return acc, total

        acc, total = lax.fori_loop(
            0,
            cols_n // plan_w,
            over_cols,
            (jnp.zeros((qw, LABELS), F32), jnp.zeros((qw, 128), F32)),
        )
        lanes[rows, :] = total
        return acc

    sent = []
    for d in range(1, nr):
        owner = lax.rem(own_r + d, nr)
        lsend[d] = label_mass(owner)
        copy = pltpu.make_async_remote_copy(
            src_ref=lsend.at[d],
            dst_ref=lbuf.at[d],
            send_sem=l_send.at[d],
            recv_sem=l_recv.at[d],
            device_id={"ref": owner},
            device_id_type=MESH,
        )
        copy.start()
        sent.append(copy)
    own_mass = label_mass(own_r)
    copies = swap_rows(ITERS, to_row(lanes[...], jnp.sum))
    qpot_ref[...] = (query_base + jnp.log2(row_scale)) * (1.0 / SCALE) + q_norm * (1.0 / PCA)
    rpot_ref[...] = (jnp.log2(col_scale) - peak[...]) * (1.0 / SCALE)
    for copy in copies:
        copy.wait()
    lanes[...] = from_row(1.0 / total_of(rbuf, ITERS, nr))
    for copy in sent:
        copy.wait()
    for d in range(1, nr):
        own_mass = own_mass + lbuf[d]
    inverse = lanes[pl.ds(pl.multiple_of(own_r * qw, qw), qw), :]
    for t in range(LABELS // 128):
        probs_ref[:, t * 128 : (t + 1) * 128] = own_mass[:, t * 128 : (t + 1) * 128] * inverse


def per_device(query_features, ref_features, query_blocks, ref_blocks, ref_labels, cluster_pairs):
    nq = lax.axis_size("query")
    nr = lax.axis_size("ref")
    qw = query_features.shape[1]
    rw = ref_features.shape[1]
    rows_n, cols_n = qw * nr, rw * nq
    dma = pltpu.SemaphoreType.DMA
    vmem = pl.BlockSpec(memory_space=pltpu.VMEM)
    smem = pl.BlockSpec(memory_space=pltpu.SMEM)
    probs, qpot, rpot = pl.pallas_call(
        functools.partial(kernel, nq, nr),
        out_shape=(
            jax.ShapeDtypeStruct((qw, LABELS), F32),
            jax.ShapeDtypeStruct((1, rows_n), F32),
            jax.ShapeDtypeStruct((1, cols_n), F32),
        ),
        in_specs=[vmem, vmem, vmem, smem, smem, smem],
        out_specs=(vmem, vmem, vmem),
        scratch_shapes=[
            pltpu.VMEM((nr, PCA, qw), BF16),
            pltpu.VMEM((DEPTH, cols_n), BF16),
            pltpu.VMEM((rows_n, DEPTH), BF16),
            pltpu.VMEM((rows_n, cols_n), F32),
            pltpu.VMEM((LABELS, cols_n), BF16),
            pltpu.VMEM((rows_n, 128), F32),
            pltpu.VMEM((rows_n, 128), F32),
            pltpu.VMEM((1, cols_n), F32),
            pltpu.VMEM((1, cols_n), F32),
            pltpu.VMEM((1, cols_n), F32),
            pltpu.VMEM((ITERS + 1, nr, 1, rows_n), F32),
            pltpu.VMEM((ITERS, nq, 1, cols_n), F32),
            pltpu.VMEM((nr, qw, LABELS), F32),
            pltpu.VMEM((nr, qw, LABELS), F32),
            dma((nr,)), dma((nr,)),
            dma((nq,)), dma((nq,)), dma((nq,)), dma((nq,)),
            dma((ITERS + 1, nr)), dma((ITERS + 1, nr)),
            dma((ITERS, nq)), dma((ITERS, nq)),
            dma((nr,)), dma((nr,)),
        ],
        compiler_params=pltpu.CompilerParams(
            collective_id=0, has_side_effects=True, vmem_limit_bytes=56 * 1024 * 1024
        ),
    )(
        query_features, ref_features, ref_labels.reshape(1, -1), query_blocks.reshape(1, -1),
        ref_blocks.reshape(1, -1), cluster_pairs,
    )
    return probs, qpot.reshape(-1), rpot.reshape(-1)


def solution(mesh):
    in_specs = (
        P(None, ("groups", "query", "ref")),
        P(None, ("groups", "ref", "query")),
        P(("groups", "query")),
        P(("groups", "ref")),
        P(("groups", "ref")),
        P("groups", None),
    )
    out_specs = (P(("groups", "query", "ref"), None), P(("groups", "query")), P(("groups", "ref")))
    return jax.shard_map(
        per_device, mesh=mesh, in_specs=in_specs, out_specs=out_specs, check_vma=False
    )
```

```python
import functools
import math

import jax
import jax.numpy as jnp
from jax import lax
from jax.experimental import pallas as pl
from jax.experimental.pallas import tpu as pltpu
from jax.sharding import PartitionSpec as P

PCA = 64
LABELS = 256
CB = 64
ITERS = 3
EPS = 0.002

SCALE = math.log2(math.e) / EPS
DOT_SCALE = 2.0 * SCALE / PCA
BLOCKED = -(2.0**100)
FLOOR = -1e20
TINY = 1e-37
DEPTH = 128
MESH = pl.DeviceIdType.MESH
F32 = jnp.float32
BF16 = jnp.bfloat16


def to_row(lanes, reduce):
    return reduce(lanes.T, axis=0, keepdims=True)


def from_row(row):
    return jnp.broadcast_to(row, (128, row.shape[1])).T


def kernel(
    nq, nr, q_ref, r_ref, labels_in, qb_in, rb_in, pairs_in,
    probs_out, qpot_out, rpot_out,
    labels_ref, qb_ref, rb_ref, pairs_ref, probs_ref, qpot_ref, rpot_ref, partial, mass_sum,
    qg, aug_r, aug_q, scores, onehot, lanes, spread, peak, share, scale_row,
    rbuf, cbuf, lbuf, lsend,
    q_send, q_recv, r_send, r_recv, f_send, f_recv, row_send, row_recv, col_send, col_recv,
    l_send, l_recv, in_sem, out_sem,
):
    own_q = lax.axis_index("query")
    own_r = lax.axis_index("ref")
    qw = q_ref.shape[1]
    rw = r_ref.shape[1]
    rows_n = qw * nr
    cols_n = rw * nq
    chips = nq // 2
    core = lax.rem(own_q, 2)
    chip = own_q // 2
    sibling = chip * 2 + (1 - core)
    log_query = math.log2(rows_n * nq)
    log_ref = math.log2(cols_n * nr)

    def block_cols(owner, width):
        return pl.ds(pl.multiple_of(owner * width, 128), width)

    fills = [
        pltpu.make_async_copy(source, target, in_sem.at[k])
        for k, (source, target) in enumerate(
            [
                (r_ref, aug_r.at[pl.ds(0, PCA), block_cols(own_q, rw)]),
                (q_ref, qg.at[own_r]),
                (labels_in, labels_ref),
                (qb_in, qb_ref),
                (rb_in, rb_ref),
                (pairs_in, pairs_ref),
            ]
        )
    ]
    for fill in fills:
        fill.start()
    barrier = pltpu.get_barrier_semaphore()
    for d in range(1, nq):
        pl.semaphore_signal(
            barrier, inc=1, device_id={"query": lax.rem(own_q + d, nq)}, device_id_type=MESH
        )
    for d in range(1, nr):
        pl.semaphore_signal(
            barrier, inc=1, device_id={"ref": lax.rem(own_r + d, nr)}, device_id_type=MESH
        )
    pl.semaphore_wait(barrier, nq + nr - 2)

    half_w = rw // 2
    q_copies = []
    r_copies = {}

    def piece_of(owner, part):
        return aug_r.at[
            pl.ds(0, PCA), pl.ds(pl.multiple_of(owner * rw + part * half_w, 128), half_w)
        ]

    for part in range(2):
        for d in range(1, chips):
            copy = pltpu.make_async_remote_copy(
                src_ref=r_ref.at[:, pl.ds(part * half_w, half_w)],
                dst_ref=piece_of(own_q, part),
                send_sem=r_send.at[part, d],
                recv_sem=r_recv.at[part, d],
                device_id={"query": lax.rem(chip + d, chips) * 2 + core},
                device_id_type=MESH,
            )
            copy.start()
            r_copies[part, d] = copy
    sibling_copy = pltpu.make_async_remote_copy(
        src_ref=r_ref,
        dst_ref=aug_r.at[pl.ds(0, PCA), block_cols(own_q, rw)],
        send_sem=r_send.at[0, 0],
        recv_sem=r_recv.at[0, 0],
        device_id={"query": sibling},
        device_id_type=MESH,
    )
    sibling_copy.start()
    for d in range(1, nr):
        q_copies.append(
            pltpu.make_async_remote_copy(
                src_ref=q_ref,
                dst_ref=qg.at[own_r],
                send_sem=q_send.at[d],
                recv_sem=q_recv.at[d],
                device_id={"ref": lax.rem(own_r + d, nr)},
                device_id_type=MESH,
            )
        )
        q_copies[-1].start()

    aug_r[pl.ds(80, DEPTH - 80), :] = jnp.zeros((DEPTH - 80, cols_n), BF16)

    for fill in fills:
        fill.wait()
    sub = lax.broadcasted_iota(jnp.int32, (8, 128), 0)
    lane = lax.broadcasted_iota(jnp.int32, (8, 128), 1)

    parts = []
    for k in range(rows_n // 128):
        cluster = jnp.where(lane < CB, qb_ref[0, 2 * k], qb_ref[0, 2 * k + 1])
        hit = jnp.zeros((8, 128), F32)
        for p in range(pairs_ref.shape[1]):
            both = jnp.logical_and(sub == pairs_ref[1, p], cluster == pairs_ref[0, p])
            hit = jnp.where(both, 1.0, hit)
        parts.append(jnp.where(hit > 0.5, 0.0, BLOCKED))
    blocked = jnp.concatenate(parts, axis=1)

    label_id = lax.broadcasted_iota(jnp.int32, (LABELS, 128), 0)

    def label_step(k, carry):
        cols = pl.ds(pl.multiple_of(k * 128, 128), 128)
        onehot[:, cols] = jnp.where(label_id == labels_ref[:, cols], 1.0, 0.0).astype(BF16)
        return carry

    lax.fori_loop(0, cols_n // 128, label_step, 0, unroll=2)

    for copy in q_copies:
        copy.wait()
    q_cols = jnp.concatenate([qg[k].astype(F32) for k in range(nr)], axis=1)
    q_norm = jnp.sum(q_cols * q_cols, axis=0, keepdims=True)
    filler = jnp.concatenate(
        [jnp.full((3, rows_n), -1.0, F32), jnp.zeros((DEPTH - PCA - 11, rows_n), F32)], axis=0
    )
    aug_q[...] = jnp.concatenate([q_cols, blocked, filler], axis=0).T.astype(BF16)

    lanes[...] = jnp.full((rows_n, 128), -3e38, F32)
    step_w = 256
    row_t = 128

    def score_block(base, width):

        def score_step(j, carry):
            cols = pl.ds(pl.multiple_of(base + j * step_w, 128), step_w)
            piece = aug_r[pl.ds(0, PCA), cols].astype(F32)
            half = 0.5 * jnp.sum(piece * piece, axis=0, keepdims=True)
            high = half.astype(BF16).astype(F32)
            middle = (half - high).astype(BF16).astype(F32)
            low = half - high - middle
            ids = []
            for t in range(step_w // 128):
                at = (base + j * step_w) // CB + 2 * t
                cluster = jnp.where(lane < CB, rb_ref[0, at], rb_ref[0, at + 1])
                ids.append(jnp.where(sub == cluster, 1.0, 0.0))
            extra = jnp.concatenate(
                [jnp.concatenate(ids, axis=1), high, middle, low, jnp.zeros((5, step_w), F32)],
                axis=0,
            )
            aug_r[pl.ds(PCA, 16), cols] = extra.astype(BF16)
            right = aug_r[:, cols]
            for i in range(rows_n // row_t):
                rows = pl.ds(i * row_t, row_t)
                value = DOT_SCALE * jnp.dot(aug_q[rows, :], right, preferred_element_type=F32)
                scores[rows, cols] = value
                top = lanes[rows, :]
                for t in range(step_w // 128):
                    top = jnp.maximum(top, value[:, t * 128 : (t + 1) * 128])
                lanes[rows, :] = top
            return carry

        lax.fori_loop(0, width // step_w, score_step, 0)

    score_block(own_q * rw, rw)
    sibling_copy.wait()
    score_block(sibling * rw, rw)
    for part in range(2):
        handed = []
        for d in range(1, chips):
            r_copies[part, d].wait()
            block = piece_of(lax.rem(chip + chips - d, chips) * 2 + core, part)
            copy = pltpu.make_async_remote_copy(
                src_ref=block,
                dst_ref=block,
                send_sem=f_send.at[part, d],
                recv_sem=f_recv.at[part, d],
                device_id={"query": sibling},
                device_id_type=MESH,
            )
            copy.start()
            handed.append(copy)
        for d in range(1, chips):
            owner = lax.rem(chip + chips - d, chips) * 2 + core
            score_block(owner * rw + part * half_w, half_w)
        for d in range(1, chips):
            handed[d - 1].wait()
            owner = lax.rem(chip + chips - d, chips) * 2 + 1 - core
            score_block(owner * rw + part * half_w, half_w)

    def swap(buf, stage, send, recv, axis, own, count):
        copies = []
        for d in range(1, count):
            copies.append(
                pltpu.make_async_remote_copy(
                    src_ref=buf.at[stage, own],
                    dst_ref=buf.at[stage, own],
                    send_sem=send.at[stage, d],
                    recv_sem=recv.at[stage, d],
                    device_id={axis: lax.rem(own + d, count)},
                    device_id_type=MESH,
                )
            )
            copies[-1].start()
        return copies

    def swap_rows(stage, row):
        rbuf[stage, own_r] = row
        return swap(rbuf, stage, row_send, row_recv, "ref", own_r, nr)

    def swap_cols(stage, row):
        cbuf[stage, own_q] = row
        return swap(cbuf, stage, col_send, col_recv, "query", own_q, nq)

    def total_of(buf, stage, count):
        total = buf[stage, 0]
        for k in range(1, count):
            total = total + buf[stage, k]
        return total

    def joined(buf, stage, count):
        top = buf[stage, 0]
        for k in range(1, count):
            top = jnp.maximum(top, buf[stage, k])
        mass = jnp.exp2(buf[stage, 0] - top)
        for k in range(1, count):
            mass = mass + jnp.exp2(buf[stage, k] - top)
        return top, mass

    row_b = 64
    lane_steps = 8

    def row_sweep(term, bound):
        def over_rows(i, carry):
            rows = pl.ds(pl.multiple_of(i * row_b, row_b), row_b)
            held = bound[rows, :] if bound is not None else None

            def over_cols(j, acc):
                for t in range(lane_steps):
                    at = pl.multiple_of((j * lane_steps + t) * 128, 128)
                    acc = acc + term(rows, pl.ds(at, 128), held)
                return acc

            lanes[rows, :] = lax.fori_loop(
                0, cols_n // (128 * lane_steps), over_cols, jnp.zeros((row_b, 128), F32)
            )
            return carry

        lax.fori_loop(0, rows_n // row_b, over_rows, 0)
        return to_row(lanes[...], jnp.sum)

    top = jnp.maximum(to_row(lanes[...], jnp.max), FLOOR)
    spread[...] = from_row(top)
    mass = row_sweep(lambda rows, cols, held: jnp.exp2(scores[rows, cols] - held), spread)
    for copy in swap_rows(0, top + jnp.log2(jnp.maximum(mass, TINY))):
        copy.wait()
    top, mass = joined(rbuf, 0, nr)
    query_base = -log_query - (top + jnp.log2(mass))
    spread[...] = from_row(query_base)

    col_w = 512

    def lane_starts(j):
        return [pl.multiple_of(j * col_w + t * 128, 128) for t in range(col_w // 128)]

    def squeeze(target, reduce):
        def squeeze_step(j, carry):
            for at in lane_starts(j):
                target[:, pl.ds(at, 128)] = reduce(partial[:, pl.ds(at, 128)], axis=0, keepdims=True)
            return carry

        lax.fori_loop(0, cols_n // col_w, squeeze_step, 0, unroll=2)

    def column_top(j, carry):
        starts = lane_starts(j)
        tops = [jnp.full((8, 128), FLOOR, F32) for _ in starts]
        for i in range(rows_n // row_b):
            rows = pl.ds(i * row_b, row_b)
            base = spread[rows, :]
            for t, at in enumerate(starts):
                value = scores[rows, pl.ds(at, 128)] + base
                tops[t] = jnp.maximum(
                    tops[t], jnp.max(value.reshape(row_b // 8, 8, 128), axis=0)
                )
        for t, at in enumerate(starts):
            partial[:, pl.ds(at, 128)] = tops[t]
        return carry

    def column_first(j, carry):
        starts = lane_starts(j)
        tops = [jnp.broadcast_to(peak[:, pl.ds(at, 128)], (8, 128)) for at in starts]
        sums = [jnp.zeros((8, 128), F32) for _ in starts]
        for i in range(rows_n // row_b):
            rows = pl.ds(i * row_b, row_b)
            base = spread[rows, :].reshape(row_b // 8, 8, 128)
            for t, at in enumerate(starts):
                value = scores[rows, pl.ds(at, 128)].reshape(row_b // 8, 8, 128)
                value = jnp.exp2(value + base - tops[t][None])
                scores[rows, pl.ds(at, 128)] = value.reshape(row_b, 128)
                sums[t] = sums[t] + jnp.sum(value, axis=0)
        for t, at in enumerate(starts):
            partial[:, pl.ds(at, 128)] = sums[t]
        return carry

    lax.fori_loop(0, cols_n // col_w, column_top, 0)
    squeeze(peak, jnp.max)
    lax.fori_loop(0, cols_n // col_w, column_first, 0)
    squeeze(share, jnp.sum)
    for copy in swap_cols(0, peak[...] + jnp.log2(jnp.maximum(share[...], TINY))):
        copy.wait()
    top, mass = joined(cbuf, 0, nq)
    share[...] = jnp.exp2(peak[...] - top)
    peak[...] = top
    scale_row[...] = share[...] * (2.0**-log_ref) / mass

    for step in range(1, ITERS):
        part = row_sweep(lambda rows, cols, held: scores[rows, cols] * scale_row[:, cols], None)
        for copy in swap_rows(step, part):
            copy.wait()
        row_scale = 2.0**-log_query / total_of(rbuf, step, nr)
        spread[...] = from_row(row_scale)

        def column_later(j, carry):
            starts = lane_starts(j)
            sums = [jnp.zeros((8, 128), F32) for _ in starts]
            for i in range(rows_n // row_b):
                rows = pl.ds(i * row_b, row_b)
                factor = spread[rows, :]
                for t, at in enumerate(starts):
                    value = scores[rows, pl.ds(at, 128)] * factor
                    sums[t] = sums[t] + jnp.sum(value.reshape(row_b // 8, 8, 128), axis=0)
            for t, at in enumerate(starts):
                partial[:, pl.ds(at, 128)] = sums[t]
            return carry

        lax.fori_loop(0, cols_n // col_w, column_later, 0)
        squeeze(scale_row, jnp.sum)
        for copy in swap_cols(step, share[...] * scale_row[...]):
            copy.wait()
        col_scale = 2.0**-log_ref / total_of(cbuf, step, nq)
        scale_row[...] = share[...] * col_scale

    qpot_ref[...] = (query_base + jnp.log2(row_scale)) * (1.0 / SCALE) + q_norm * (1.0 / PCA)
    rpot_ref[...] = (jnp.log2(col_scale) - peak[...]) * (1.0 / SCALE)
    stores = [
        pltpu.make_async_copy(qpot_ref, qpot_out, out_sem.at[0]),
        pltpu.make_async_copy(rpot_ref, rpot_out, out_sem.at[1]),
    ]
    for store in stores:
        store.start()

    plan_w = 512
    near = nr // 2
    half_rows = qw * near
    place = lax.rem(own_r, near)
    near_base = own_r - place
    far_base = lax.rem(near_base + near, nr)
    lanes[...] = jnp.zeros_like(lanes)

    def label_mass(base):
        rows = pl.ds(pl.multiple_of(base * qw, half_rows), half_rows)
        mass_sum[...] = jnp.zeros_like(mass_sum)

        def over_cols(j, carry):
            pieces = []
            factor = spread[rows, :]
            total = lanes[rows, :]
            for t in range(plan_w // 128):
                cols = pl.ds(pl.multiple_of(j * plan_w + t * 128, 128), 128)
                value = scores[rows, cols] * (factor * scale_row[:, cols])
                total = total + value
                pieces.append(value.astype(BF16))
            lanes[rows, :] = total
            marks = onehot[:, pl.ds(pl.multiple_of(j * plan_w, 128), plan_w)]
            mass_sum[...] += lax.dot_general(
                jnp.concatenate(pieces, axis=1),
                marks,
                (((1,), (1,)), ((), ())),
                preferred_element_type=F32,
            )
            return carry

        lax.fori_loop(0, cols_n // plan_w, over_cols, 0)

    sent = []

    def hand_out(base, slot, k):
        at = lax.rem(place + k, near)
        lsend[slot] = mass_sum[pl.ds(pl.multiple_of(at * qw, qw), qw), :].astype(BF16)
        copy = pltpu.make_async_remote_copy(
            src_ref=lsend.at[slot],
            dst_ref=lbuf.at[slot],
            send_sem=l_send.at[slot],
            recv_sem=l_recv.at[slot],
            device_id={"ref": base + at},
            device_id_type=MESH,
        )
        copy.start()
        sent.append(copy)

    label_mass(far_base)
    for k in range(near):
        hand_out(far_base, near + k, k)
    label_mass(near_base)
    for k in range(1, near):
        hand_out(near_base, k, k)
    copies = swap_rows(ITERS, to_row(lanes[...], jnp.sum))
    own_mass = mass_sum[pl.ds(pl.multiple_of(place * qw, qw), qw), :]
    for copy in copies:
        copy.wait()
    lanes[...] = from_row(1.0 / total_of(rbuf, ITERS, nr))
    for copy in reversed(sent):
        copy.wait()
    for d in range(1, nr):
        own_mass = own_mass + lbuf[d].astype(F32)
    inverse = lanes[pl.ds(pl.multiple_of(own_r * qw, qw), qw), :]
    for t in range(LABELS // 128):
        probs_ref[:, t * 128 : (t + 1) * 128] = own_mass[:, t * 128 : (t + 1) * 128] * inverse
    last = pltpu.make_async_copy(probs_ref, probs_out, out_sem.at[2])
    last.start()
    for store in stores:
        store.wait()
    last.wait()


def per_device(query_features, ref_features, query_blocks, ref_blocks, ref_labels, cluster_pairs):
    nq = lax.axis_size("query")
    nr = lax.axis_size("ref")
    qw = query_features.shape[1]
    rw = ref_features.shape[1]
    rows_n, cols_n = qw * nr, rw * nq
    dma = pltpu.SemaphoreType.DMA
    anywhere = pl.BlockSpec(memory_space=pl.ANY)
    pairs_n = cluster_pairs.shape[0]
    probs, qpot, rpot = pl.pallas_call(
        functools.partial(kernel, nq, nr),
        out_shape=(
            jax.ShapeDtypeStruct((qw, LABELS), F32),
            jax.ShapeDtypeStruct((1, rows_n), F32),
            jax.ShapeDtypeStruct((1, cols_n), F32),
        ),
        in_specs=[anywhere] * 6,
        out_specs=(anywhere, anywhere, anywhere),
        scratch_shapes=[
            pltpu.VMEM((1, cols_n), jnp.int32),
            pltpu.SMEM((1, query_blocks.shape[0]), jnp.int32),
            pltpu.SMEM((1, ref_blocks.shape[0]), jnp.int32),
            pltpu.SMEM((2, pairs_n), jnp.int32),
            pltpu.VMEM((qw, LABELS), F32),
            pltpu.VMEM((1, rows_n), F32),
            pltpu.VMEM((1, cols_n), F32),
            pltpu.VMEM((8, cols_n), F32),
            pltpu.VMEM((rows_n // 2, LABELS), F32),
            pltpu.VMEM((nr, PCA, qw), BF16),
            pltpu.VMEM((DEPTH, cols_n), BF16),
            pltpu.VMEM((rows_n, DEPTH), BF16),
            pltpu.VMEM((rows_n, cols_n), F32),
            pltpu.VMEM((LABELS, cols_n), BF16),
            pltpu.VMEM((rows_n, 128), F32),
            pltpu.VMEM((rows_n, 128), F32),
            pltpu.VMEM((1, cols_n), F32),
            pltpu.VMEM((1, cols_n), F32),
            pltpu.VMEM((1, cols_n), F32),
            pltpu.VMEM((ITERS + 1, nr, 1, rows_n), F32),
            pltpu.VMEM((ITERS, nq, 1, cols_n), F32),
            pltpu.VMEM((nr, qw, LABELS), BF16),
            pltpu.VMEM((nr, qw, LABELS), BF16),
            dma((nr,)), dma((nr,)),
            dma((2, nq)), dma((2, nq)), dma((2, nq)), dma((2, nq)),
            dma((ITERS + 1, nr)), dma((ITERS + 1, nr)),
            dma((ITERS, nq)), dma((ITERS, nq)),
            dma((nr,)), dma((nr,)), dma((6,)), dma((3,)),
        ],
        compiler_params=pltpu.CompilerParams(
            collective_id=0, has_side_effects=True, vmem_limit_bytes=56 * 1024 * 1024
        ),
    )(
        query_features, ref_features, ref_labels.reshape(1, -1), query_blocks.reshape(1, -1),
        ref_blocks.reshape(1, -1), cluster_pairs.T,
    )
    return probs, qpot.reshape(-1), rpot.reshape(-1)


def solution(mesh):
    in_specs = (
        P(None, ("groups", "query", "ref")),
        P(None, ("groups", "ref", "query")),
        P(("groups", "query")),
        P(("groups", "ref")),
        P(("groups", "ref")),
        P("groups", None),
    )
    out_specs = (P(("groups", "query", "ref"), None), P(("groups", "query")), P(("groups", "ref")))
    return jax.shard_map(
        per_device, mesh=mesh, in_specs=in_specs, out_specs=out_specs, check_vma=False
    )
```

```python
import functools
import math

import jax
import jax.numpy as jnp
from jax import lax
from jax.experimental import pallas as pl
from jax.experimental.pallas import tpu as pltpu
from jax.sharding import PartitionSpec as P

PCA = 64
LABELS = 256
CB = 64
ITERS = 3
EPS = 0.002

SCALE = math.log2(math.e) / EPS
DOT_SCALE = 2.0 * SCALE / PCA
BLOCKED = -(2.0**100)
FLOOR = -1e20
TINY = 1e-37
DEPTH = 128
MESH = pl.DeviceIdType.MESH
F32 = jnp.float32
BF16 = jnp.bfloat16


def to_row(lanes, reduce):
    return reduce(lanes.T, axis=0, keepdims=True)


def from_row(row):
    return jnp.broadcast_to(row, (128, row.shape[1])).T


def kernel(
    nq, nr, q_ref, r_ref, labels_in, qb_in, rb_in, pairs_in,
    probs_out, qpot_out, rpot_out,
    labels_ref, qb_ref, rb_ref, pairs_ref, probs_ref, qpot_ref, rpot_ref, partial, mass_sum, ratios,
    qg, aug_r, aug_q, scores, onehot, lanes, spread, peak, share, scale_row,
    rbuf, cbuf, lbuf, lsend,
    q_send, q_recv, r_send, r_recv, f_send, f_recv, row_send, row_recv, col_send, col_recv,
    l_send, l_recv, in_sem, out_sem,
):
    own_q = lax.axis_index("query")
    own_r = lax.axis_index("ref")
    qw = q_ref.shape[1]
    rw = r_ref.shape[1]
    rows_n = qw * nr
    cols_n = rw * nq
    chips = nq // 2
    core = lax.rem(own_q, 2)
    chip = own_q // 2
    sibling = chip * 2 + (1 - core)
    log_query = math.log2(rows_n * nq)
    log_ref = math.log2(cols_n * nr)

    def block_cols(owner, width):
        return pl.ds(pl.multiple_of(owner * width, 128), width)

    fills = [
        pltpu.make_async_copy(source, target, in_sem.at[k])
        for k, (source, target) in enumerate(
            [
                (r_ref, aug_r.at[pl.ds(0, PCA), block_cols(own_q, rw)]),
                (q_ref, qg.at[own_r]),
                (labels_in, labels_ref),
                (qb_in, qb_ref),
                (rb_in, rb_ref),
                (pairs_in, pairs_ref),
            ]
        )
    ]
    for fill in fills:
        fill.start()
    barrier = pltpu.get_barrier_semaphore()
    for d in range(1, nq):
        pl.semaphore_signal(
            barrier, inc=1, device_id={"query": lax.rem(own_q + d, nq)}, device_id_type=MESH
        )
    for d in range(1, nr):
        pl.semaphore_signal(
            barrier, inc=1, device_id={"ref": lax.rem(own_r + d, nr)}, device_id_type=MESH
        )
    pl.semaphore_wait(barrier, nq + nr - 2)

    half_w = rw // 2
    q_copies = []
    r_copies = {}

    def piece_of(owner, part):
        return aug_r.at[
            pl.ds(0, PCA), pl.ds(pl.multiple_of(owner * rw + part * half_w, 128), half_w)
        ]

    for part in range(2):
        for d in range(1, chips):
            copy = pltpu.make_async_remote_copy(
                src_ref=r_ref.at[:, pl.ds(part * half_w, half_w)],
                dst_ref=piece_of(own_q, part),
                send_sem=r_send.at[part, d],
                recv_sem=r_recv.at[part, d],
                device_id={"query": lax.rem(chip + d, chips) * 2 + core},
                device_id_type=MESH,
            )
            copy.start()
            r_copies[part, d] = copy
    sibling_copy = pltpu.make_async_remote_copy(
        src_ref=r_ref,
        dst_ref=aug_r.at[pl.ds(0, PCA), block_cols(own_q, rw)],
        send_sem=r_send.at[0, 0],
        recv_sem=r_recv.at[0, 0],
        device_id={"query": sibling},
        device_id_type=MESH,
    )
    sibling_copy.start()
    for d in range(1, nr):
        q_copies.append(
            pltpu.make_async_remote_copy(
                src_ref=q_ref,
                dst_ref=qg.at[own_r],
                send_sem=q_send.at[d],
                recv_sem=q_recv.at[d],
                device_id={"ref": lax.rem(own_r + d, nr)},
                device_id_type=MESH,
            )
        )
        q_copies[-1].start()

    aug_r[pl.ds(80, DEPTH - 80), :] = jnp.zeros((DEPTH - 80, cols_n), BF16)

    for fill in fills:
        fill.wait()
    sub = lax.broadcasted_iota(jnp.int32, (8, 128), 0)
    lane = lax.broadcasted_iota(jnp.int32, (8, 128), 1)

    parts = []
    for k in range(rows_n // 128):
        cluster = jnp.where(lane < CB, qb_ref[0, 2 * k], qb_ref[0, 2 * k + 1])
        hit = jnp.zeros((8, 128), F32)
        for p in range(pairs_ref.shape[1]):
            both = jnp.logical_and(sub == pairs_ref[1, p], cluster == pairs_ref[0, p])
            hit = jnp.where(both, 1.0, hit)
        parts.append(jnp.where(hit > 0.5, 0.0, BLOCKED))
    blocked = jnp.concatenate(parts, axis=1)

    label_id = lax.broadcasted_iota(jnp.int32, (LABELS, 128), 0)

    def label_step(k, carry):
        cols = pl.ds(pl.multiple_of(k * 128, 128), 128)
        onehot[:, cols] = jnp.where(label_id == labels_ref[:, cols], 1.0, 0.0).astype(BF16)
        return carry

    lax.fori_loop(0, cols_n // 128, label_step, 0, unroll=2)

    for copy in q_copies:
        copy.wait()
    q_cols = jnp.concatenate([qg[k].astype(F32) for k in range(nr)], axis=1)
    q_norm = jnp.sum(q_cols * q_cols, axis=0, keepdims=True)
    filler = jnp.concatenate(
        [jnp.full((3, rows_n), -1.0, F32), jnp.zeros((DEPTH - PCA - 11, rows_n), F32)], axis=0
    )
    aug_q[...] = jnp.concatenate([q_cols, blocked, filler], axis=0).T.astype(BF16)

    lanes[...] = jnp.full((rows_n, 128), -3e38, F32)
    step_w = 256
    row_t = 128

    def score_block(base, width):

        def score_step(j, carry):
            cols = pl.ds(pl.multiple_of(base + j * step_w, 128), step_w)
            piece = aug_r[pl.ds(0, PCA), cols].astype(F32)
            half = 0.5 * jnp.sum(piece * piece, axis=0, keepdims=True)
            high = half.astype(BF16).astype(F32)
            middle = (half - high).astype(BF16).astype(F32)
            low = half - high - middle
            ids = []
            for t in range(step_w // 128):
                at = (base + j * step_w) // CB + 2 * t
                cluster = jnp.where(lane < CB, rb_ref[0, at], rb_ref[0, at + 1])
                ids.append(jnp.where(sub == cluster, 1.0, 0.0))
            extra = jnp.concatenate(
                [jnp.concatenate(ids, axis=1), high, middle, low, jnp.zeros((5, step_w), F32)],
                axis=0,
            )
            aug_r[pl.ds(PCA, 16), cols] = extra.astype(BF16)
            right = aug_r[:, cols]
            for i in range(rows_n // row_t):
                rows = pl.ds(i * row_t, row_t)
                value = DOT_SCALE * jnp.dot(aug_q[rows, :], right, preferred_element_type=F32)
                scores[rows, cols] = value
                top = lanes[rows, :]
                for t in range(step_w // 128):
                    top = jnp.maximum(top, value[:, t * 128 : (t + 1) * 128])
                lanes[rows, :] = top
            return carry

        lax.fori_loop(0, width // step_w, score_step, 0)

    score_block(own_q * rw, rw)
    sibling_copy.wait()
    score_block(sibling * rw, rw)
    for part in range(2):
        handed = []
        for d in range(1, chips):
            r_copies[part, d].wait()
            block = piece_of(lax.rem(chip + chips - d, chips) * 2 + core, part)
            copy = pltpu.make_async_remote_copy(
                src_ref=block,
                dst_ref=block,
                send_sem=f_send.at[part, d],
                recv_sem=f_recv.at[part, d],
                device_id={"query": sibling},
                device_id_type=MESH,
            )
            copy.start()
            handed.append(copy)
        for d in range(1, chips):
            owner = lax.rem(chip + chips - d, chips) * 2 + core
            score_block(owner * rw + part * half_w, half_w)
        for d in range(1, chips):
            handed[d - 1].wait()
            owner = lax.rem(chip + chips - d, chips) * 2 + 1 - core
            score_block(owner * rw + part * half_w, half_w)

    def swap(buf, stage, send, recv, axis, own, count):
        copies = []
        for d in range(1, count):
            copies.append(
                pltpu.make_async_remote_copy(
                    src_ref=buf.at[stage, own],
                    dst_ref=buf.at[stage, own],
                    send_sem=send.at[stage, d],
                    recv_sem=recv.at[stage, d],
                    device_id={axis: lax.rem(own + d, count)},
                    device_id_type=MESH,
                )
            )
            copies[-1].start()
        return copies

    def swap_rows(stage, row):
        rbuf[stage, own_r] = row
        return swap(rbuf, stage, row_send, row_recv, "ref", own_r, nr)

    def swap_cols(stage, row):
        cbuf[stage, own_q] = row
        return swap(cbuf, stage, col_send, col_recv, "query", own_q, nq)

    def total_of(buf, stage, count):
        total = buf[stage, 0]
        for k in range(1, count):
            total = total + buf[stage, k]
        return total

    def joined(buf, stage, count):
        top = buf[stage, 0]
        for k in range(1, count):
            top = jnp.maximum(top, buf[stage, k])
        mass = jnp.exp2(buf[stage, 0] - top)
        for k in range(1, count):
            mass = mass + jnp.exp2(buf[stage, k] - top)
        return top, mass

    row_b = 64
    lane_steps = 8

    def row_sweep(term, bound):
        def over_rows(i, carry):
            rows = pl.ds(pl.multiple_of(i * row_b, row_b), row_b)
            held = bound[rows, :] if bound is not None else None

            def over_cols(j, acc):
                for t in range(lane_steps):
                    at = pl.multiple_of((j * lane_steps + t) * 128, 128)
                    acc = acc + term(rows, pl.ds(at, 128), held)
                return acc

            lanes[rows, :] = lax.fori_loop(
                0, cols_n // (128 * lane_steps), over_cols, jnp.zeros((row_b, 128), F32)
            )
            return carry

        lax.fori_loop(0, rows_n // row_b, over_rows, 0)
        return to_row(lanes[...], jnp.sum)

    top = jnp.maximum(to_row(lanes[...], jnp.max), FLOOR)
    spread[...] = from_row(top)
    mass = row_sweep(lambda rows, cols, held: jnp.exp2(scores[rows, cols] - held), spread)
    for copy in swap_rows(0, top + jnp.log2(jnp.maximum(mass, TINY))):
        copy.wait()
    top, mass = joined(rbuf, 0, nr)
    query_base = -log_query - (top + jnp.log2(mass))
    spread[...] = from_row(query_base)

    col_w = 512

    def lane_starts(j):
        return [pl.multiple_of(j * col_w + t * 128, 128) for t in range(col_w // 128)]

    def squeeze(target, reduce):
        def squeeze_step(j, carry):
            for at in lane_starts(j):
                target[:, pl.ds(at, 128)] = reduce(partial[:, pl.ds(at, 128)], axis=0, keepdims=True)
            return carry

        lax.fori_loop(0, cols_n // col_w, squeeze_step, 0, unroll=2)

    def column_top(j, carry):
        starts = lane_starts(j)
        tops = [jnp.full((8, 128), FLOOR, F32) for _ in starts]
        for i in range(rows_n // row_b):
            rows = pl.ds(i * row_b, row_b)
            base = spread[rows, :]
            for t, at in enumerate(starts):
                value = scores[rows, pl.ds(at, 128)] + base
                tops[t] = jnp.maximum(
                    tops[t], jnp.max(value.reshape(row_b // 8, 8, 128), axis=0)
                )
        for t, at in enumerate(starts):
            partial[:, pl.ds(at, 128)] = tops[t]
        return carry

    def column_first(j, carry):
        starts = lane_starts(j)
        tops = [jnp.broadcast_to(peak[:, pl.ds(at, 128)], (8, 128)) for at in starts]
        sums = [jnp.zeros((8, 128), F32) for _ in starts]
        for i in range(rows_n // row_b):
            rows = pl.ds(i * row_b, row_b)
            base = spread[rows, :].reshape(row_b // 8, 8, 128)
            for t, at in enumerate(starts):
                value = scores[rows, pl.ds(at, 128)].reshape(row_b // 8, 8, 128)
                value = jnp.exp2(value + base - tops[t][None])
                ratios[rows, pl.ds(at, 128)] = value.reshape(row_b, 128)
                sums[t] = sums[t] + jnp.sum(value, axis=0)
        for t, at in enumerate(starts):
            partial[:, pl.ds(at, 128)] = sums[t]
        return carry

    lax.fori_loop(0, cols_n // col_w, column_top, 0)
    squeeze(peak, jnp.max)
    lax.fori_loop(0, cols_n // col_w, column_first, 0)
    squeeze(share, jnp.sum)
    for copy in swap_cols(0, peak[...] + jnp.log2(jnp.maximum(share[...], TINY))):
        copy.wait()
    top, mass = joined(cbuf, 0, nq)
    share[...] = jnp.exp2(peak[...] - top)
    peak[...] = top
    scale_row[...] = share[...] * (2.0**-log_ref) / mass

    for step in range(1, ITERS):
        part = row_sweep(lambda rows, cols, held: ratios[rows, cols] * scale_row[:, cols], None)
        for copy in swap_rows(step, part):
            copy.wait()
        row_scale = 2.0**-log_query / total_of(rbuf, step, nr)
        spread[...] = from_row(row_scale)

        def column_later(j, carry):
            starts = lane_starts(j)
            sums = [jnp.zeros((8, 128), F32) for _ in starts]
            for i in range(rows_n // row_b):
                rows = pl.ds(i * row_b, row_b)
                factor = spread[rows, :]
                for t, at in enumerate(starts):
                    value = ratios[rows, pl.ds(at, 128)] * factor
                    sums[t] = sums[t] + jnp.sum(value.reshape(row_b // 8, 8, 128), axis=0)
            for t, at in enumerate(starts):
                partial[:, pl.ds(at, 128)] = sums[t]
            return carry

        lax.fori_loop(0, cols_n // col_w, column_later, 0)
        squeeze(scale_row, jnp.sum)
        for copy in swap_cols(step, share[...] * scale_row[...]):
            copy.wait()
        col_scale = 2.0**-log_ref / total_of(cbuf, step, nq)
        scale_row[...] = share[...] * col_scale

    qpot_ref[...] = (query_base + jnp.log2(row_scale)) * (1.0 / SCALE) + q_norm * (1.0 / PCA)
    rpot_ref[...] = (jnp.log2(col_scale) - peak[...]) * (1.0 / SCALE)
    stores = [
        pltpu.make_async_copy(qpot_ref, qpot_out, out_sem.at[0]),
        pltpu.make_async_copy(rpot_ref, rpot_out, out_sem.at[1]),
    ]
    for store in stores:
        store.start()

    plan_w = 512
    near = nr // 2
    half_rows = qw * near
    place = lax.rem(own_r, near)
    near_base = own_r - place
    far_base = lax.rem(near_base + near, nr)
    lanes[...] = jnp.zeros_like(lanes)

    def label_mass(base):
        rows = pl.ds(pl.multiple_of(base * qw, half_rows), half_rows)
        mass_sum[...] = jnp.zeros_like(mass_sum)

        def over_cols(j, carry):
            pieces = []
            factor = spread[rows, :]
            total = lanes[rows, :]
            for t in range(plan_w // 128):
                cols = pl.ds(pl.multiple_of(j * plan_w + t * 128, 128), 128)
                value = ratios[rows, cols] * (factor * scale_row[:, cols])
                total = total + value
                pieces.append(value.astype(BF16))
            lanes[rows, :] = total
            marks = onehot[:, pl.ds(pl.multiple_of(j * plan_w, 128), plan_w)]
            mass_sum[...] += lax.dot_general(
                jnp.concatenate(pieces, axis=1),
                marks,
                (((1,), (1,)), ((), ())),
                preferred_element_type=F32,
            )
            return carry

        lax.fori_loop(0, cols_n // plan_w, over_cols, 0)

    sent = []

    def hand_out(base, slot, k):
        at = lax.rem(place + k, near)
        lsend[slot] = mass_sum[pl.ds(pl.multiple_of(at * qw, qw), qw), :].astype(BF16)
        copy = pltpu.make_async_remote_copy(
            src_ref=lsend.at[slot],
            dst_ref=lbuf.at[slot],
            send_sem=l_send.at[slot],
            recv_sem=l_recv.at[slot],
            device_id={"ref": base + at},
            device_id_type=MESH,
        )
        copy.start()
        sent.append(copy)

    label_mass(far_base)
    for k in range(near):
        hand_out(far_base, near + k, k)
    label_mass(near_base)
    for k in range(1, near):
        hand_out(near_base, k, k)
    copies = swap_rows(ITERS, to_row(lanes[...], jnp.sum))
    own_mass = mass_sum[pl.ds(pl.multiple_of(place * qw, qw), qw), :]
    for copy in copies:
        copy.wait()
    lanes[...] = from_row(1.0 / total_of(rbuf, ITERS, nr))
    for copy in reversed(sent):
        copy.wait()
    for d in range(1, nr):
        own_mass = own_mass + lbuf[d].astype(F32)
    inverse = lanes[pl.ds(pl.multiple_of(own_r * qw, qw), qw), :]
    for t in range(LABELS // 128):
        probs_ref[:, t * 128 : (t + 1) * 128] = own_mass[:, t * 128 : (t + 1) * 128] * inverse
    last = pltpu.make_async_copy(probs_ref, probs_out, out_sem.at[2])
    last.start()
    for store in stores:
        store.wait()
    last.wait()


def per_device(query_features, ref_features, query_blocks, ref_blocks, ref_labels, cluster_pairs):
    nq = lax.axis_size("query")
    nr = lax.axis_size("ref")
    qw = query_features.shape[1]
    rw = ref_features.shape[1]
    rows_n, cols_n = qw * nr, rw * nq
    dma = pltpu.SemaphoreType.DMA
    anywhere = pl.BlockSpec(memory_space=pl.ANY)
    pairs_n = cluster_pairs.shape[0]
    probs, qpot, rpot = pl.pallas_call(
        functools.partial(kernel, nq, nr),
        out_shape=(
            jax.ShapeDtypeStruct((qw, LABELS), F32),
            jax.ShapeDtypeStruct((1, rows_n), F32),
            jax.ShapeDtypeStruct((1, cols_n), F32),
        ),
        in_specs=[anywhere] * 6,
        out_specs=(anywhere, anywhere, anywhere),
        scratch_shapes=[
            pltpu.VMEM((1, cols_n), jnp.int32),
            pltpu.SMEM((1, query_blocks.shape[0]), jnp.int32),
            pltpu.SMEM((1, ref_blocks.shape[0]), jnp.int32),
            pltpu.SMEM((2, pairs_n), jnp.int32),
            pltpu.VMEM((qw, LABELS), F32),
            pltpu.VMEM((1, rows_n), F32),
            pltpu.VMEM((1, cols_n), F32),
            pltpu.VMEM((8, cols_n), F32),
            pltpu.VMEM((rows_n // 2, LABELS), F32),
            pltpu.VMEM((rows_n, cols_n), F32),
            pltpu.VMEM((nr, PCA, qw), BF16),
            pltpu.VMEM((DEPTH, cols_n), BF16),
            pltpu.VMEM((rows_n, DEPTH), BF16),
            pltpu.VMEM((rows_n, cols_n), F32),
            pltpu.VMEM((LABELS, cols_n), BF16),
            pltpu.VMEM((rows_n, 128), F32),
            pltpu.VMEM((rows_n, 128), F32),
            pltpu.VMEM((1, cols_n), F32),
            pltpu.VMEM((1, cols_n), F32),
            pltpu.VMEM((1, cols_n), F32),
            pltpu.VMEM((ITERS + 1, nr, 1, rows_n), F32),
            pltpu.VMEM((ITERS, nq, 1, cols_n), F32),
            pltpu.VMEM((nr, qw, LABELS), BF16),
            pltpu.VMEM((nr, qw, LABELS), BF16),
            dma((nr,)), dma((nr,)),
            dma((2, nq)), dma((2, nq)), dma((2, nq)), dma((2, nq)),
            dma((ITERS + 1, nr)), dma((ITERS + 1, nr)),
            dma((ITERS, nq)), dma((ITERS, nq)),
            dma((nr,)), dma((nr,)), dma((6,)), dma((3,)),
        ],
        compiler_params=pltpu.CompilerParams(
            collective_id=0, has_side_effects=True, vmem_limit_bytes=56 * 1024 * 1024
        ),
    )(
        query_features, ref_features, ref_labels.reshape(1, -1), query_blocks.reshape(1, -1),
        ref_blocks.reshape(1, -1), cluster_pairs.T,
    )
    return probs, qpot.reshape(-1), rpot.reshape(-1)


def solution(mesh):
    in_specs = (
        P(None, ("groups", "query", "ref")),
        P(None, ("groups", "ref", "query")),
        P(("groups", "query")),
        P(("groups", "ref")),
        P(("groups", "ref")),
        P("groups", None),
    )
    out_specs = (P(("groups", "query", "ref"), None), P(("groups", "query")), P(("groups", "ref")))
    return jax.shard_map(
        per_device, mesh=mesh, in_specs=in_specs, out_specs=out_specs, check_vma=False
    )
```

```python
import functools
import math

import jax
import jax.numpy as jnp
from jax import lax
from jax.experimental import pallas as pl
from jax.experimental.pallas import tpu as pltpu
from jax.sharding import PartitionSpec as P

PCA = 64
LABELS = 256
CB = 64
ITERS = 3
EPS = 0.002

SCALE = math.log2(math.e) / EPS
DOT_SCALE = 2.0 * SCALE / PCA
BLOCKED = -(2.0**100)
FLOOR = -1e20
TINY = 1e-37
DEPTH = 128
MESH = pl.DeviceIdType.MESH
F32 = jnp.float32
BF16 = jnp.bfloat16


def to_row(lanes, reduce):
    return reduce(lanes.T, axis=0, keepdims=True)


def from_row(row):
    return jnp.broadcast_to(row, (128, row.shape[1])).T


def kernel(
    nq, nr, q_ref, r_ref, labels_in, qb_in, rb_in, pairs_in,
    probs_out, qpot_out, rpot_out,
    labels_ref, qb_ref, rb_ref, pairs_ref, probs_ref, qpot_ref, rpot_ref, partial, mass_sum, ratios,
    qg, aug_r, aug_q, scores, onehot, lanes, spread, peak, share, scale_row,
    rbuf, cbuf, lbuf, lsend,
    q_send, q_recv, r_send, r_recv, f_send, f_recv, row_send, row_recv, col_send, col_recv,
    l_send, l_recv, in_sem, out_sem,
):
    own_q = lax.axis_index("query")
    own_r = lax.axis_index("ref")
    qw = q_ref.shape[1]
    rw = r_ref.shape[1]
    rows_n = qw * nr
    cols_n = rw * nq
    chips = nq // 2
    core = lax.rem(own_q, 2)
    chip = own_q // 2
    sibling = chip * 2 + (1 - core)
    log_query = math.log2(rows_n * nq)
    log_ref = math.log2(cols_n * nr)

    def block_cols(owner, width):
        return pl.ds(pl.multiple_of(owner * width, 128), width)

    fills = [
        pltpu.make_async_copy(source, target, in_sem.at[k])
        for k, (source, target) in enumerate(
            [
                (r_ref, aug_r.at[pl.ds(0, PCA), block_cols(own_q, rw)]),
                (q_ref, qg.at[own_r]),
                (labels_in, labels_ref),
                (qb_in, qb_ref),
                (rb_in, rb_ref),
                (pairs_in, pairs_ref),
            ]
        )
    ]
    for fill in fills:
        fill.start()
    barrier = pltpu.get_barrier_semaphore()
    for d in range(1, nq):
        pl.semaphore_signal(
            barrier, inc=1, device_id={"query": lax.rem(own_q + d, nq)}, device_id_type=MESH
        )
    for d in range(1, nr):
        pl.semaphore_signal(
            barrier, inc=1, device_id={"ref": lax.rem(own_r + d, nr)}, device_id_type=MESH
        )
    pl.semaphore_wait(barrier, nq + nr - 2)

    half_w = rw // 2
    q_copies = []
    r_copies = {}

    def piece_of(owner, part):
        return aug_r.at[
            pl.ds(0, PCA), pl.ds(pl.multiple_of(owner * rw + part * half_w, 128), half_w)
        ]

    for part in range(2):
        for d in range(1, chips):
            copy = pltpu.make_async_remote_copy(
                src_ref=r_ref.at[:, pl.ds(part * half_w, half_w)],
                dst_ref=piece_of(own_q, part),
                send_sem=r_send.at[part, d],
                recv_sem=r_recv.at[part, d],
                device_id={"query": lax.rem(chip + d, chips) * 2 + core},
                device_id_type=MESH,
            )
            copy.start()
            r_copies[part, d] = copy
    sibling_copy = pltpu.make_async_remote_copy(
        src_ref=r_ref,
        dst_ref=aug_r.at[pl.ds(0, PCA), block_cols(own_q, rw)],
        send_sem=r_send.at[0, 0],
        recv_sem=r_recv.at[0, 0],
        device_id={"query": sibling},
        device_id_type=MESH,
    )
    sibling_copy.start()
    for d in range(1, nr):
        q_copies.append(
            pltpu.make_async_remote_copy(
                src_ref=q_ref,
                dst_ref=qg.at[own_r],
                send_sem=q_send.at[d],
                recv_sem=q_recv.at[d],
                device_id={"ref": lax.rem(own_r + d, nr)},
                device_id_type=MESH,
            )
        )
        q_copies[-1].start()

    aug_r[pl.ds(80, DEPTH - 80), :] = jnp.zeros((DEPTH - 80, cols_n), BF16)

    for fill in fills:
        fill.wait()
    sub = lax.broadcasted_iota(jnp.int32, (8, 128), 0)
    lane = lax.broadcasted_iota(jnp.int32, (8, 128), 1)

    parts = []
    for k in range(rows_n // 128):
        cluster = jnp.where(lane < CB, qb_ref[0, 2 * k], qb_ref[0, 2 * k + 1])
        hit = jnp.zeros((8, 128), F32)
        for p in range(pairs_ref.shape[1]):
            both = jnp.logical_and(sub == pairs_ref[1, p], cluster == pairs_ref[0, p])
            hit = jnp.where(both, 1.0, hit)
        parts.append(jnp.where(hit > 0.5, 0.0, BLOCKED))
    blocked = jnp.concatenate(parts, axis=1)

    label_id = lax.broadcasted_iota(jnp.int32, (LABELS, 128), 0)

    def label_step(k, carry):
        cols = pl.ds(pl.multiple_of(k * 128, 128), 128)
        onehot[:, cols] = jnp.where(label_id == labels_ref[:, cols], 1.0, 0.0).astype(BF16)
        return carry

    lax.fori_loop(0, cols_n // 128, label_step, 0, unroll=2)

    for copy in q_copies:
        copy.wait()
    q_cols = jnp.concatenate([qg[k].astype(F32) for k in range(nr)], axis=1)
    q_norm = jnp.sum(q_cols * q_cols, axis=0, keepdims=True)
    filler = jnp.concatenate(
        [jnp.full((3, rows_n), -1.0, F32), jnp.zeros((DEPTH - PCA - 11, rows_n), F32)], axis=0
    )
    aug_q[...] = jnp.concatenate([q_cols, blocked, filler], axis=0).T.astype(BF16)

    lanes[...] = jnp.full((rows_n, 128), -3e38, F32)
    step_w = 512
    row_t = 128

    def score_block(base, width):

        def score_step(j, carry):
            cols = pl.ds(pl.multiple_of(base + j * step_w, 128), step_w)
            piece = aug_r[pl.ds(0, PCA), cols].astype(F32)
            half = 0.5 * jnp.sum(piece * piece, axis=0, keepdims=True)
            high = half.astype(BF16).astype(F32)
            middle = (half - high).astype(BF16).astype(F32)
            low = half - high - middle
            ids = []
            for t in range(step_w // 128):
                at = (base + j * step_w) // CB + 2 * t
                cluster = jnp.where(lane < CB, rb_ref[0, at], rb_ref[0, at + 1])
                ids.append(jnp.where(sub == cluster, 1.0, 0.0))
            extra = jnp.concatenate(
                [jnp.concatenate(ids, axis=1), high, middle, low, jnp.zeros((5, step_w), F32)],
                axis=0,
            )
            aug_r[pl.ds(PCA, 16), cols] = extra.astype(BF16)
            right = aug_r[:, cols]
            for i in range(rows_n // row_t):
                rows = pl.ds(i * row_t, row_t)
                value = DOT_SCALE * jnp.dot(aug_q[rows, :], right, preferred_element_type=F32)
                scores[rows, cols] = value
                top = lanes[rows, :]
                for t in range(step_w // 128):
                    top = jnp.maximum(top, value[:, t * 128 : (t + 1) * 128])
                lanes[rows, :] = top
            return carry

        lax.fori_loop(0, width // step_w, score_step, 0)

    score_block(own_q * rw, rw)
    sibling_copy.wait()
    score_block(sibling * rw, rw)
    for part in range(2):
        handed = []
        for d in range(1, chips):
            r_copies[part, d].wait()
            block = piece_of(lax.rem(chip + chips - d, chips) * 2 + core, part)
            copy = pltpu.make_async_remote_copy(
                src_ref=block,
                dst_ref=block,
                send_sem=f_send.at[part, d],
                recv_sem=f_recv.at[part, d],
                device_id={"query": sibling},
                device_id_type=MESH,
            )
            copy.start()
            handed.append(copy)
        for d in range(1, chips):
            owner = lax.rem(chip + chips - d, chips) * 2 + core
            score_block(owner * rw + part * half_w, half_w)
        for d in range(1, chips):
            handed[d - 1].wait()
            owner = lax.rem(chip + chips - d, chips) * 2 + 1 - core
            score_block(owner * rw + part * half_w, half_w)

    def swap(buf, stage, send, recv, axis, own, count):
        copies = []
        for d in range(1, count):
            copies.append(
                pltpu.make_async_remote_copy(
                    src_ref=buf.at[stage, own],
                    dst_ref=buf.at[stage, own],
                    send_sem=send.at[stage, d],
                    recv_sem=recv.at[stage, d],
                    device_id={axis: lax.rem(own + d, count)},
                    device_id_type=MESH,
                )
            )
            copies[-1].start()
        return copies

    def swap_rows(stage, row):
        rbuf[stage, own_r] = row
        return swap(rbuf, stage, row_send, row_recv, "ref", own_r, nr)

    def swap_cols(stage, row):
        cbuf[stage, own_q] = row
        return swap(cbuf, stage, col_send, col_recv, "query", own_q, nq)

    def total_of(buf, stage, count):
        total = buf[stage, 0]
        for k in range(1, count):
            total = total + buf[stage, k]
        return total

    def joined(buf, stage, count):
        top = buf[stage, 0]
        for k in range(1, count):
            top = jnp.maximum(top, buf[stage, k])
        mass = jnp.exp2(buf[stage, 0] - top)
        for k in range(1, count):
            mass = mass + jnp.exp2(buf[stage, k] - top)
        return top, mass

    row_b = 64
    lane_steps = 8

    def row_sweep(term, bound):
        def over_rows(i, carry):
            rows = pl.ds(pl.multiple_of(i * row_b, row_b), row_b)
            held = bound[rows, :] if bound is not None else None

            def over_cols(j, acc):
                for t in range(lane_steps):
                    at = pl.multiple_of((j * lane_steps + t) * 128, 128)
                    acc = acc + term(rows, pl.ds(at, 128), held)
                return acc

            lanes[rows, :] = lax.fori_loop(
                0, cols_n // (128 * lane_steps), over_cols, jnp.zeros((row_b, 128), F32)
            )
            return carry

        lax.fori_loop(0, rows_n // row_b, over_rows, 0)
        return to_row(lanes[...], jnp.sum)

    top = jnp.maximum(to_row(lanes[...], jnp.max), FLOOR)
    spread[...] = from_row(top)
    mass = row_sweep(lambda rows, cols, held: jnp.exp2(scores[rows, cols] - held), spread)
    for copy in swap_rows(0, top + jnp.log2(jnp.maximum(mass, TINY))):
        copy.wait()
    top, mass = joined(rbuf, 0, nr)
    query_base = -log_query - (top + jnp.log2(mass))
    spread[...] = from_row(query_base)

    col_w = 512

    def lane_starts(j):
        return [pl.multiple_of(j * col_w + t * 128, 128) for t in range(col_w // 128)]

    def squeeze(target, reduce):
        def squeeze_step(j, carry):
            for at in lane_starts(j):
                target[:, pl.ds(at, 128)] = reduce(partial[:, pl.ds(at, 128)], axis=0, keepdims=True)
            return carry

        lax.fori_loop(0, cols_n // col_w, squeeze_step, 0, unroll=2)

    def column_top(j, carry):
        starts = lane_starts(j)
        tops = [jnp.full((8, 128), FLOOR, F32) for _ in starts]
        for i in range(rows_n // row_b):
            rows = pl.ds(i * row_b, row_b)
            base = spread[rows, :]
            for t, at in enumerate(starts):
                value = scores[rows, pl.ds(at, 128)] + base
                tops[t] = jnp.maximum(
                    tops[t], jnp.max(value.reshape(row_b // 8, 8, 128), axis=0)
                )
        for t, at in enumerate(starts):
            partial[:, pl.ds(at, 128)] = tops[t]
        return carry

    def column_first(j, carry):
        starts = lane_starts(j)
        tops = [jnp.broadcast_to(peak[:, pl.ds(at, 128)], (8, 128)) for at in starts]
        sums = [jnp.zeros((8, 128), F32) for _ in starts]
        for i in range(rows_n // row_b):
            rows = pl.ds(i * row_b, row_b)
            base = spread[rows, :].reshape(row_b // 8, 8, 128)
            for t, at in enumerate(starts):
                value = scores[rows, pl.ds(at, 128)].reshape(row_b // 8, 8, 128)
                value = jnp.exp2(value + base - tops[t][None])
                ratios[rows, pl.ds(at, 128)] = value.reshape(row_b, 128)
                sums[t] = sums[t] + jnp.sum(value, axis=0)
        for t, at in enumerate(starts):
            partial[:, pl.ds(at, 128)] = sums[t]
        return carry

    lax.fori_loop(0, cols_n // col_w, column_top, 0)
    squeeze(peak, jnp.max)
    lax.fori_loop(0, cols_n // col_w, column_first, 0)
    squeeze(share, jnp.sum)
    for copy in swap_cols(0, peak[...] + jnp.log2(jnp.maximum(share[...], TINY))):
        copy.wait()
    top, mass = joined(cbuf, 0, nq)
    share[...] = jnp.exp2(peak[...] - top)
    peak[...] = top
    scale_row[...] = share[...] * (2.0**-log_ref) / mass

    for step in range(1, ITERS):
        part = row_sweep(lambda rows, cols, held: ratios[rows, cols] * scale_row[:, cols], None)
        for copy in swap_rows(step, part):
            copy.wait()
        row_scale = 2.0**-log_query / total_of(rbuf, step, nr)
        spread[...] = from_row(row_scale)

        def column_later(j, carry):
            starts = lane_starts(j)
            sums = [jnp.zeros((8, 128), F32) for _ in starts]
            for i in range(rows_n // row_b):
                rows = pl.ds(i * row_b, row_b)
                factor = spread[rows, :]
                for t, at in enumerate(starts):
                    value = ratios[rows, pl.ds(at, 128)] * factor
                    sums[t] = sums[t] + jnp.sum(value.reshape(row_b // 8, 8, 128), axis=0)
            for t, at in enumerate(starts):
                partial[:, pl.ds(at, 128)] = sums[t]
            return carry

        lax.fori_loop(0, cols_n // col_w, column_later, 0)
        squeeze(scale_row, jnp.sum)
        for copy in swap_cols(step, share[...] * scale_row[...]):
            copy.wait()
        col_scale = 2.0**-log_ref / total_of(cbuf, step, nq)
        scale_row[...] = share[...] * col_scale

    qpot_ref[...] = (query_base + jnp.log2(row_scale)) * (1.0 / SCALE) + q_norm * (1.0 / PCA)
    rpot_ref[...] = (jnp.log2(col_scale) - peak[...]) * (1.0 / SCALE)
    stores = [
        pltpu.make_async_copy(qpot_ref, qpot_out, out_sem.at[0]),
        pltpu.make_async_copy(rpot_ref, rpot_out, out_sem.at[1]),
    ]
    for store in stores:
        store.start()

    plan_w = 2048
    near = nr // 2
    half_rows = qw * near
    place = lax.rem(own_r, near)
    near_base = own_r - place
    far_base = lax.rem(near_base + near, nr)
    lanes[...] = jnp.zeros_like(lanes)

    def label_mass(base):
        rows = pl.ds(pl.multiple_of(base * qw, half_rows), half_rows)
        mass_sum[...] = jnp.zeros_like(mass_sum)

        def over_cols(j, carry):
            pieces = []
            factor = spread[rows, :]
            total = lanes[rows, :]
            for t in range(plan_w // 128):
                cols = pl.ds(pl.multiple_of(j * plan_w + t * 128, 128), 128)
                value = ratios[rows, cols] * (factor * scale_row[:, cols])
                total = total + value
                pieces.append(value.astype(BF16))
            lanes[rows, :] = total
            marks = onehot[:, pl.ds(pl.multiple_of(j * plan_w, 128), plan_w)]
            mass_sum[...] += lax.dot_general(
                jnp.concatenate(pieces, axis=1),
                marks,
                (((1,), (1,)), ((), ())),
                preferred_element_type=F32,
            )
            return carry

        lax.fori_loop(0, cols_n // plan_w, over_cols, 0)

    sent = []

    def hand_out(base, slot, k):
        at = lax.rem(place + k, near)
        lsend[slot] = mass_sum[pl.ds(pl.multiple_of(at * qw, qw), qw), :].astype(BF16)
        copy = pltpu.make_async_remote_copy(
            src_ref=lsend.at[slot],
            dst_ref=lbuf.at[slot],
            send_sem=l_send.at[slot],
            recv_sem=l_recv.at[slot],
            device_id={"ref": base + at},
            device_id_type=MESH,
        )
        copy.start()
        sent.append(copy)

    label_mass(far_base)
    for k in range(near):
        hand_out(far_base, near + k, k)
    label_mass(near_base)
    for k in range(1, near):
        hand_out(near_base, k, k)
    copies = swap_rows(ITERS, to_row(lanes[...], jnp.sum))
    own_mass = mass_sum[pl.ds(pl.multiple_of(place * qw, qw), qw), :]
    for copy in copies:
        copy.wait()
    lanes[...] = from_row(1.0 / total_of(rbuf, ITERS, nr))
    for copy in reversed(sent):
        copy.wait()
    for d in range(1, nr):
        own_mass = own_mass + lbuf[d].astype(F32)
    inverse = lanes[pl.ds(pl.multiple_of(own_r * qw, qw), qw), :]
    for t in range(LABELS // 128):
        probs_ref[:, t * 128 : (t + 1) * 128] = own_mass[:, t * 128 : (t + 1) * 128] * inverse
    last = pltpu.make_async_copy(probs_ref, probs_out, out_sem.at[2])
    last.start()
    for store in stores:
        store.wait()
    last.wait()


def per_device(query_features, ref_features, query_blocks, ref_blocks, ref_labels, cluster_pairs):
    nq = lax.axis_size("query")
    nr = lax.axis_size("ref")
    qw = query_features.shape[1]
    rw = ref_features.shape[1]
    rows_n, cols_n = qw * nr, rw * nq
    dma = pltpu.SemaphoreType.DMA
    anywhere = pl.BlockSpec(memory_space=pl.ANY)
    pairs_n = cluster_pairs.shape[0]
    probs, qpot, rpot = pl.pallas_call(
        functools.partial(kernel, nq, nr),
        out_shape=(
            jax.ShapeDtypeStruct((qw, LABELS), F32),
            jax.ShapeDtypeStruct((1, rows_n), F32),
            jax.ShapeDtypeStruct((1, cols_n), F32),
        ),
        in_specs=[anywhere] * 6,
        out_specs=(anywhere, anywhere, anywhere),
        scratch_shapes=[
            pltpu.VMEM((1, cols_n), jnp.int32),
            pltpu.SMEM((1, query_blocks.shape[0]), jnp.int32),
            pltpu.SMEM((1, ref_blocks.shape[0]), jnp.int32),
            pltpu.SMEM((2, pairs_n), jnp.int32),
            pltpu.VMEM((qw, LABELS), F32),
            pltpu.VMEM((1, rows_n), F32),
            pltpu.VMEM((1, cols_n), F32),
            pltpu.VMEM((8, cols_n), F32),
            pltpu.VMEM((rows_n // 2, LABELS), F32),
            pltpu.VMEM((rows_n, cols_n), F32),
            pltpu.VMEM((nr, PCA, qw), BF16),
            pltpu.VMEM((DEPTH, cols_n), BF16),
            pltpu.VMEM((rows_n, DEPTH), BF16),
            pltpu.VMEM((rows_n, cols_n), F32),
            pltpu.VMEM((LABELS, cols_n), BF16),
            pltpu.VMEM((rows_n, 128), F32),
            pltpu.VMEM((rows_n, 128), F32),
            pltpu.VMEM((1, cols_n), F32),
            pltpu.VMEM((1, cols_n), F32),
            pltpu.VMEM((1, cols_n), F32),
            pltpu.VMEM((ITERS + 1, nr, 1, rows_n), F32),
            pltpu.VMEM((ITERS, nq, 1, cols_n), F32),
            pltpu.VMEM((nr, qw, LABELS), BF16),
            pltpu.VMEM((nr, qw, LABELS), BF16),
            dma((nr,)), dma((nr,)),
            dma((2, nq)), dma((2, nq)), dma((2, nq)), dma((2, nq)),
            dma((ITERS + 1, nr)), dma((ITERS + 1, nr)),
            dma((ITERS, nq)), dma((ITERS, nq)),
            dma((nr,)), dma((nr,)), dma((6,)), dma((3,)),
        ],
        compiler_params=pltpu.CompilerParams(
            collective_id=0, has_side_effects=True, vmem_limit_bytes=56 * 1024 * 1024
        ),
    )(
        query_features, ref_features, ref_labels.reshape(1, -1), query_blocks.reshape(1, -1),
        ref_blocks.reshape(1, -1), cluster_pairs.T,
    )
    return probs, qpot.reshape(-1), rpot.reshape(-1)


def solution(mesh):
    in_specs = (
        P(None, ("groups", "query", "ref")),
        P(None, ("groups", "ref", "query")),
        P(("groups", "query")),
        P(("groups", "ref")),
        P(("groups", "ref")),
        P("groups", None),
    )
    out_specs = (P(("groups", "query", "ref"), None), P(("groups", "query")), P(("groups", "ref")))
    return jax.shard_map(
        per_device, mesh=mesh, in_specs=in_specs, out_specs=out_specs, check_vma=False
    )
```
